128 devices in a mesh: bx: 16 (over x, y_lo, core), by: 8 (over y_hi, z).
Axes of the slice: x: 4, y: 4 (y_hi: 2, y_lo: 2; y = y_hi * 2 + y_lo), z: 4, core: 2. Of those that a mesh axis runs over, the one named last changes fastest.
Arguments:
- coeffs: bfloat16 [2, 4096, 16, 8, 256], P(None, None, 'bx', 'by'), may hold values from -6 to 6
- interp: bfloat16 [8, 2, 2, 256, 256], replicated, may hold values from -0.25 to 0.25
- src_grid: int32 [256], replicated, may hold values from 0 to 4095
- tgt_grid: int32 [8, 16, 8], replicated, may hold values from 0 to 4095
Outputs:
- result: bfloat16 [2, 4096, 16, 8, 256], P(None, None, 'bx', 'by')
The draws below stay inside these ranges and needn't reach their ends.
All inputs are finite; a program needn't handle non-finite values.
Results may differ from the reference program's by a relative error of at most 0.02.
Values may be sent and summed in bfloat16 or wider, within the bound.
A program may use at most 128 MiB of HBM per device.

```python
import math
import jax
import jax.numpy as jnp
import numpy as np

K = 256
GRID = 4096
LEVELS = 8
R = 4096
N_BX = 16
N_BY = 8


def touch_ends(values, rng, smallest, largest):
    longest = values.shape.index(max(values.shape))
    spots = []
    for shift in (0, 1):
        where = [jax.random.randint(jax.random.fold_in(rng, axis), (), 0, length) for axis, length in enumerate(values.shape)]
        where[longest] = (where[longest] + shift) % values.shape[longest]
        spots.append(tuple(where))
    return values.at[spots[0]].set(smallest).at[spots[1]].set(largest)


def levels(key, extent, cuts, least, largest):
    level = 1.0
    for dim, shards_of in cuts:
        draws = jax.random.uniform(jax.random.fold_in(jax.random.fold_in(key, 6), dim), (shards_of,), jnp.float32, least / len(cuts), largest / len(cuts))
        level = level * jnp.repeat(jnp.exp(draws), extent[dim] // shards_of).reshape((-1,) + (1,) * (len(extent) - 1 - dim))
    return level


def scatter_about(own_key, extent, deviation, limit, cuts=(), held_as=jnp.bfloat16):
    level = levels(own_key, extent, cuts, -0.22, 0.18) if cuts else 1.0
    array = jax.random.normal(own_key, extent, jnp.float32) * deviation * level
    return jnp.minimum(jnp.maximum(array, -limit), limit).astype(held_as)


def setup_inputs(seed: int = 0) -> dict:
    seeds = jax.random.split(jax.random.key(seed), 5)
    coeffs = scatter_about(seeds[0], (2, R, N_BX, N_BY, K), 1.0, 6.0, ((2, 16), (3, 8)))
    interp = scatter_about(seeds[1], (LEVELS, 2, 2, K, K), (2 * K) ** -0.5, 0.25)
    src_grid = touch_ends(jax.random.randint(seeds[2], (K,), 0, GRID), jax.random.fold_in(seeds[2], 1), 0, GRID - 1).astype(jnp.int32)
    tgt_grid = touch_ends(jax.random.randint(seeds[3], (LEVELS, N_BX, N_BY), 0, GRID), jax.random.fold_in(seeds[3], 1), 0, GRID - 1).astype(jnp.int32)
    return dict(coeffs=coeffs, interp=interp, src_grid=src_grid, tgt_grid=tgt_grid)


def reference(coeffs, interp, src_grid, tgt_grid):
    state = coeffs
    for level in range(LEVELS):
        count = N_BX if level % 2 == 0 else N_BY
        bit = (level // 2) % (count.bit_length() - 1)
        index = np.arange(count)
        partner_idx = index ^ (1 << bit)
        child = (index >> bit) & 1
        axis = 2 if level % 2 == 0 else 3
        partner = jnp.take(state, jnp.asarray(partner_idx, jnp.int32), axis=axis)
        weights = interp[level].astype(jnp.float32)
        own_mat = weights[child, child]
        other_mat = weights[child, 1 - child]
        form = "zrabj,ajk->zrabk" if level % 2 == 0 else "zrabj,bjk->zrabk"
        total = jnp.einsum(form, state.astype(jnp.float32), own_mat) + jnp.einsum(form, partner.astype(jnp.float32), other_mat)
        prod = (tgt_grid[level][:, :, None] * src_grid[None, None, :]) % GRID
        theta = (2.0 * math.pi / GRID) * prod.astype(jnp.float32)
        cosine = jnp.cos(theta)
        sine = jnp.sin(theta)
        real_new = total[0] * cosine - total[1] * sine
        imag_new = total[0] * sine + total[1] * cosine
        state = jnp.stack([real_new, imag_new]).astype(jnp.bfloat16)
    return state
```

```python
import functools
import math

import jax
import jax.numpy as jnp
from jax import lax
from jax.experimental import pallas as pl
from jax.experimental.pallas import tpu as pltpu
from jax.sharding import PartitionSpec as P

GRID = 4096
LEVELS = 8
CHUNKS = 2
GROUP = 32
PAIRS = 16
SIDE = 4
BATCH = SIDE * SIDE
BATCHES = 2 * SIDE
EARLY = 6
MESH = pl.DeviceIdType.MESH


def level_bits(n_bx, n_by):
    bits_x = n_bx.bit_length() - 1
    bits_y = n_by.bit_length() - 1
    bits = []
    for level in range(LEVELS):
        if level % 2 == 0:
            bits.append(bits_y + level // 2 % bits_x)
        else:
            bits.append(level // 2 % bits_y)
    return bits


def phases(prod):
    quadrant = (prod + GRID // 8) >> 10
    angle = (prod - (quadrant << 10)).astype(jnp.float32) * (2.0 * math.pi / GRID)
    sq = angle * angle
    cosine = 1.0 + sq * (-1 / 2 + sq * (1 / 24 + sq * (-1 / 720 + sq * (1 / 40320))))
    sine = angle * (1.0 + sq * (-1 / 6 + sq * (1 / 120 + sq * (-1 / 5040 + sq * (1 / 362880)))))
    odd = (quadrant & 1) == 1
    first = jnp.where(odd, sine, cosine)
    second = jnp.where(odd, cosine, sine)
    cos_sign = jnp.where((quadrant == 1) | (quadrant == 2), -1.0, 1.0)
    sin_sign = jnp.where((quadrant == 2) | (quadrant == 3), -1.0, 1.0)
    return first * cos_sign, second * sin_sign


def apply_level(level, bit, source, target, interp, cosine, sine):
    boxes, _, rows, width = source.shape
    stride = 1 << bit
    weights = [interp[level, child].reshape(2 * width, width) for child in range(2)]
    weights = jnp.concatenate(weights, axis=1)

    def body(group, carry):
        if stride <= GROUP:
            low = [group * (2 * GROUP) + (i // stride * 2 * stride + i % stride) for i in range(GROUP)]
        else:
            runs = stride // GROUP
            base = group // runs * (2 * stride) + group % runs * GROUP
            low = [base + i for i in range(GROUP)]
        for begin in range(0, GROUP, PAIRS):
            some = low[begin:begin + PAIRS]
            halves = []
            for child in range(2):
                parts = [source[box + child * stride].reshape(2 * rows, width) for box in some]
                halves.append(jnp.concatenate(parts, axis=0))
            operand = jnp.concatenate(halves, axis=1)
            total = jnp.dot(operand, weights, preferred_element_type=jnp.float32)
            for i, box in enumerate(some):
                for child in range(2):
                    here = box + child * stride
                    re = total[2 * i * rows:(2 * i + 1) * rows, child * width:(child + 1) * width]
                    im = total[(2 * i + 1) * rows:(2 * i + 2) * rows, child * width:(child + 1) * width]
                    c = cosine[level, pl.ds(here, 1), :]
                    s = sine[level, pl.ds(here, 1), :]
                    target[here, 0] = (re * c - im * s).astype(jnp.bfloat16)
                    target[here, 1] = (re * s + im * c).astype(jnp.bfloat16)
        return carry

    lax.fori_loop(0, boxes // 2 // GROUP, body, 0)


def kernel(
    n_bx, n_by, coeffs, interp_hbm, tgt_hbm, src_hbm, out,
    state, spare, interp, tgt, src, cosine, sine, in_send, in_recv, out_send, out_recv, load_sem,
):
    boxes = n_bx * n_by
    share = state.shape[3]
    bits = level_bits(n_bx, n_by)
    my_bx, my_by = lax.axis_index("bx"), lax.axis_index("by")
    me = my_bx * n_by + my_by
    my_x = my_bx // 4
    my_y = my_by // 4 * 2 + my_bx // 2 % 2
    my_z = my_by % 4
    my_core = my_bx % 2

    loads = [
        pltpu.make_async_copy(src_hbm, src, load_sem.at[0]),
        pltpu.make_async_copy(tgt_hbm, tgt, load_sem.at[1]),
        pltpu.make_async_copy(interp_hbm, interp, load_sem.at[2]),
    ]
    for load in loads:
        load.start()

    sign = 1 + (SIDE - 2) * my_core
    xs = [(my_x + sign * i) % SIDE * 4 for i in range(SIDE)]
    ys = [(my_y + sign * i) % SIDE for i in range(SIDE)]
    ys_bx = [y % 2 * 2 for y in ys]
    ys_by = [y // 2 * 4 for y in ys]

    def batch(number, visit):
        core = (my_core + number // SIDE) % 2
        bys = [ys_by[i] + (my_z + sign * (number + i)) % SIDE for i in range(SIDE)]
        for second in range(SIDE):
            for first in range(SIDE):
                if isinstance(number, int) and number == first == second == 0:
                    continue
                i = (first + second) % SIDE
                visit(xs[first] + ys_bx[i] + core, bys[i])

    def batches(start, stop, visit):
        if start == 0:
            batch(0, functools.partial(visit, 0))
            start = 1

        def body(number, carry):
            batch(number, functools.partial(visit, number))
            return carry

        lax.fori_loop(start, stop, body, 0)

    def rows_of(chunk, box):
        return pl.ds(pl.multiple_of((chunk * boxes + box) * share, share), share)

    def greet(number, bx, by):
        pl.semaphore_signal(barrier, inc=1, device_id=(bx, by), device_id_type=MESH)

    def scatter(chunk, number, bx, by):
        pltpu.make_async_remote_copy(
            src_ref=coeffs.at[:, rows_of(chunk, bx * n_by + by)],
            dst_ref=state.at[chunk, me],
            send_sem=in_send.at[chunk, number],
            recv_sem=in_recv.at[chunk],
            device_id=(bx, by),
            device_id_type=MESH,
        ).start()

    def give_back(chunk, number, bx, by):
        pltpu.make_async_remote_copy(
            src_ref=state.at[chunk, bx * n_by + by],
            dst_ref=out.at[:, rows_of(chunk, me)],
            send_sem=out_send.at[chunk],
            recv_sem=out_recv.at[chunk],
            device_id=(bx, by),
            device_id_type=MESH,
        ).start()

    def wait_sent(chunk, number, count):
        sent = state.at[chunk, pl.ds(0, count)]
        pltpu.make_async_copy(sent, sent, in_send.at[chunk, number]).wait()

    barrier = pltpu.get_barrier_semaphore()
    batches(0, BATCHES, greet)
    pl.semaphore_wait(barrier, boxes - 1)

    batches(0, BATCHES, functools.partial(scatter, 0))
    for chunk in range(CHUNKS):
        pltpu.make_async_copy(coeffs.at[:, rows_of(chunk, me)], state.at[chunk, me], in_recv.at[chunk]).start()

    for load in loads:
        load.wait()

    def tables(level, carry):
        columns = tgt[level]
        for bx in range(n_bx):
            prod = (columns[:, bx:bx + 1] * src[...]) & (GRID - 1)
            here = pl.ds(bx * n_by, n_by)
            cosine[level, here, :], sine[level, here, :] = phases(prod)
        return carry

    lax.fori_loop(0, LEVELS, tables, 0)

    for number in range(EARLY):
        wait_sent(0, number, BATCH - (number == 0))
    batches(0, BATCHES // 2, functools.partial(scatter, 1))
    for number in range(EARLY, BATCHES):
        wait_sent(0, number, BATCH)
    batches(BATCHES // 2, BATCHES, functools.partial(scatter, 1))

    def work(chunk, carry):
        pltpu.make_async_copy(state.at[chunk], state.at[chunk], in_recv.at[chunk]).wait()

        for level in range(LEVELS):
            buffers = (state.at[chunk], spare)
            apply_level(level, bits[level], buffers[level % 2], buffers[1 - level % 2], interp, cosine, sine)
        pltpu.make_async_copy(state.at[chunk, me], out.at[:, rows_of(chunk, me)], out_recv.at[chunk]).start()
        batches(0, BATCHES, functools.partial(give_back, chunk))
        return carry

    lax.fori_loop(0, CHUNKS, work, 0)

    for number in range(BATCHES):
        wait_sent(1, number, BATCH - (number == 0))
    for chunk in range(CHUNKS):
        whole = out.at[:, pl.ds(chunk * boxes * share, boxes * share)]
        pltpu.make_async_copy(whole, whole, out_recv.at[chunk]).wait()
        others = state.at[chunk, pl.ds(0, boxes - 1)]
        pltpu.make_async_copy(others, others, out_send.at[chunk]).wait()


def local(n_bx, n_by, coeffs, interp, src_grid, tgt_grid):
    rows, width = coeffs.shape[1], coeffs.shape[-1]
    boxes = n_bx * n_by
    share = rows // boxes // CHUNKS
    anywhere = pl.BlockSpec(memory_space=pl.ANY)
    hbm = pl.BlockSpec(memory_space=pltpu.HBM)
    table = pltpu.VMEM((LEVELS, boxes, width), jnp.float32)
    dma = pltpu.SemaphoreType.DMA
    result = pl.pallas_call(
        functools.partial(kernel, n_bx, n_by),
        out_shape=jax.ShapeDtypeStruct((2, rows, width), coeffs.dtype),
        in_specs=[hbm] * 4,
        out_specs=anywhere,
        scratch_shapes=[
            pltpu.VMEM((CHUNKS, boxes, 2, share, width), coeffs.dtype),
            pltpu.VMEM((boxes, 2, share, width), coeffs.dtype),
            pltpu.VMEM(interp.shape, interp.dtype),
            pltpu.VMEM((LEVELS, n_by, n_bx), jnp.int32),
            pltpu.VMEM((1, width), jnp.int32),
            table,
            table,
            dma((CHUNKS, BATCHES)),
            dma((CHUNKS,)),
            dma((CHUNKS,)),
            dma((CHUNKS,)),
            dma((3,)),
        ],
        compiler_params=pltpu.CompilerParams(
            collective_id=0, has_side_effects=True, vmem_limit_bytes=48 * 1024 * 1024
        ),
        cost_estimate=pl.CostEstimate(
            flops=4 * LEVELS * coeffs.size * width, bytes_accessed=16 * 2**20, transcendentals=0
        ),
        name="butterfly",
    )(
        coeffs.reshape(2, rows, width),
        interp,
        pltpu.with_memory_space_constraint(tgt_grid.transpose(0, 2, 1), pltpu.HBM),
        pltpu.with_memory_space_constraint(src_grid.reshape(1, width), pltpu.HBM),
    )
    return result.reshape(2, rows, 1, 1, width)


def solution(mesh):
    placed = (P(None, None, "bx", "by", None), P(), P(), P())
    return jax.shard_map(
        functools.partial(local, mesh.shape["bx"], mesh.shape["by"]),
        mesh=mesh,
        in_specs=placed,
        out_specs=P(None, None, "bx", "by", None),
        check_vma=False,
    )
```

```python
import functools
import math

import jax
import jax.numpy as jnp
from jax import lax
from jax.experimental import pallas as pl
from jax.experimental.pallas import tpu as pltpu
from jax.sharding import PartitionSpec as P

GRID = 4096
LEVELS = 8
CHUNKS = 2
GROUP = 32
PAIRS = 16
SIDE = 4
BATCH = SIDE * SIDE
BATCHES = 2 * SIDE
EARLY = 6
MESH = pl.DeviceIdType.MESH


def level_bits(n_bx, n_by):
    bits_x = n_bx.bit_length() - 1
    bits_y = n_by.bit_length() - 1
    bits = []
    for level in range(LEVELS):
        if level % 2 == 0:
            bits.append(bits_y + level // 2 % bits_x)
        else:
            bits.append(level // 2 % bits_y)
    return bits


def phases(prod):
    quadrant = (prod + GRID // 8) >> 10
    angle = (prod - (quadrant << 10)).astype(jnp.float32) * (2.0 * math.pi / GRID)
    sq = angle * angle
    cosine = 1.0 + sq * (-1 / 2 + sq * (1 / 24 + sq * (-1 / 720 + sq * (1 / 40320))))
    sine = angle * (1.0 + sq * (-1 / 6 + sq * (1 / 120 + sq * (-1 / 5040 + sq * (1 / 362880)))))
    odd = (quadrant & 1) == 1
    first = jnp.where(odd, sine, cosine)
    second = jnp.where(odd, cosine, sine)
    cos_sign = jnp.where((quadrant == 1) | (quadrant == 2), -1.0, 1.0)
    sin_sign = jnp.where((quadrant == 2) | (quadrant == 3), -1.0, 1.0)
    return first * cos_sign, second * sin_sign


def apply_level(level, bit, source, target, interp, cosine, sine):
    boxes, _, rows, width = source.shape
    stride = 1 << bit
    weights = [interp[level, child].reshape(2 * width, width) for child in range(2)]
    weights = jnp.concatenate(weights, axis=1)

    def body(group, carry):
        if stride <= GROUP:
            low = [group * (2 * GROUP) + (i // stride * 2 * stride + i % stride) for i in range(GROUP)]
        else:
            runs = stride // GROUP
            base = group // runs * (2 * stride) + group % runs * GROUP
            low = [base + i for i in range(GROUP)]
        for begin in range(0, GROUP, PAIRS):
            some = low[begin:begin + PAIRS]
            halves = []
            for child in range(2):
                parts = [source[box + child * stride].reshape(2 * rows, width) for box in some]
                halves.append(jnp.concatenate(parts, axis=0))
            operand = jnp.concatenate(halves, axis=1)
            total = jnp.dot(operand, weights, preferred_element_type=jnp.float32)
            for i, box in enumerate(some):
                for child in range(2):
                    here = box + child * stride
                    re = total[2 * i * rows:(2 * i + 1) * rows, child * width:(child + 1) * width]
                    im = total[(2 * i + 1) * rows:(2 * i + 2) * rows, child * width:(child + 1) * width]
                    c = cosine[level, pl.ds(here, 1), :]
                    s = sine[level, pl.ds(here, 1), :]
                    target[here, 0] = (re * c - im * s).astype(jnp.bfloat16)
                    target[here, 1] = (re * s + im * c).astype(jnp.bfloat16)
        return carry

    lax.fori_loop(0, boxes // 2 // GROUP, body, 0)


def kernel(
    n_bx, n_by, coeffs, interp_hbm, tgt_hbm, src_hbm, out,
    state, spare, interp, tgt, src, cosine, sine, in_send, in_recv, out_send, out_recv, load_sem,
):
    boxes = n_bx * n_by
    share = state.shape[3]
    bits = level_bits(n_bx, n_by)
    my_bx, my_by = lax.axis_index("bx"), lax.axis_index("by")
    me = my_bx * n_by + my_by
    my_x = my_bx // 4
    my_y = my_by // 4 * 2 + my_bx // 2 % 2
    my_z = my_by % 4
    my_core = my_bx % 2

    loads = [
        pltpu.make_async_copy(src_hbm, src, load_sem.at[0]),
        pltpu.make_async_copy(tgt_hbm, tgt, load_sem.at[1]),
        pltpu.make_async_copy(interp_hbm, interp, load_sem.at[2]),
    ]
    for load in loads:
        load.start()

    ahead = SIDE // 2 * my_core
    xs = [(my_x + ahead + i) % SIDE * 4 for i in range(SIDE)]
    ys = [(my_y + ahead + i) % SIDE for i in range(SIDE)]
    ys_bx = [y % 2 * 2 for y in ys]
    ys_by = [y // 2 * 4 for y in ys]

    def batch(number, visit):
        core = (my_core + number // SIDE) % 2
        bys = [ys_by[i] + (my_z + ahead + number + i) % SIDE for i in range(SIDE)]
        for second in range(SIDE):
            for first in range(SIDE):
                i = (first + second) % SIDE
                send = functools.partial(visit, xs[first] + ys_bx[i] + core, bys[i])
                if isinstance(number, int) and number == second == 0 and first % 2 == 0:
                    pl.when(my_core != first // 2)(send)
                else:
                    send()

    def batches(start, stop, visit):
        if start == 0:
            batch(0, functools.partial(visit, 0))
            start = 1

        def body(number, carry):
            batch(number, functools.partial(visit, number))
            return carry

        lax.fori_loop(start, stop, body, 0)

    def rows_of(chunk, box):
        return pl.ds(pl.multiple_of((chunk * boxes + box) * share, share), share)

    def greet(number, bx, by):
        pl.semaphore_signal(barrier, inc=1, device_id=(bx, by), device_id_type=MESH)

    def scatter(chunk, number, bx, by):
        pltpu.make_async_remote_copy(
            src_ref=coeffs.at[:, rows_of(chunk, bx * n_by + by)],
            dst_ref=state.at[chunk, me],
            send_sem=in_send.at[chunk, number],
            recv_sem=in_recv.at[chunk],
            device_id=(bx, by),
            device_id_type=MESH,
        ).start()

    def give_back(chunk, number, bx, by):
        pltpu.make_async_remote_copy(
            src_ref=state.at[chunk, bx * n_by + by],
            dst_ref=out.at[:, rows_of(chunk, me)],
            send_sem=out_send.at[chunk],
            recv_sem=out_recv.at[chunk],
            device_id=(bx, by),
            device_id_type=MESH,
        ).start()

    def wait_sent(chunk, number, count):
        sent = state.at[chunk, pl.ds(0, count)]
        pltpu.make_async_copy(sent, sent, in_send.at[chunk, number]).wait()

    barrier = pltpu.get_barrier_semaphore()
    batches(0, BATCHES, greet)
    pl.semaphore_wait(barrier, boxes - 1)

    batches(0, BATCHES, functools.partial(scatter, 0))
    for chunk in range(CHUNKS):
        pltpu.make_async_copy(coeffs.at[:, rows_of(chunk, me)], state.at[chunk, me], in_recv.at[chunk]).start()

    for load in loads:
        load.wait()

    def tables(level, carry):
        columns = tgt[level]
        for bx in range(n_bx):
            prod = (columns[:, bx:bx + 1] * src[...]) & (GRID - 1)
            here = pl.ds(bx * n_by, n_by)
            cosine[level, here, :], sine[level, here, :] = phases(prod)
        return carry

    lax.fori_loop(0, LEVELS, tables, 0)

    for number in range(EARLY):
        wait_sent(0, number, BATCH - (number == 0))
    batches(0, BATCHES // 2, functools.partial(scatter, 1))
    for number in range(EARLY, BATCHES):
        wait_sent(0, number, BATCH)
    batches(BATCHES // 2, BATCHES, functools.partial(scatter, 1))

    def work(chunk, carry):
        pltpu.make_async_copy(state.at[chunk], state.at[chunk], in_recv.at[chunk]).wait()

        for level in range(LEVELS):
            buffers = (state.at[chunk], spare)
            apply_level(level, bits[level], buffers[level % 2], buffers[1 - level % 2], interp, cosine, sine)
        pltpu.make_async_copy(state.at[chunk, me], out.at[:, rows_of(chunk, me)], out_recv.at[chunk]).start()
        batches(0, BATCHES, functools.partial(give_back, chunk))
        return carry

    lax.fori_loop(0, CHUNKS, work, 0)

    for number in range(BATCHES):
        wait_sent(1, number, BATCH - (number == 0))
    for chunk in range(CHUNKS):
        whole = out.at[:, pl.ds(chunk * boxes * share, boxes * share)]
        pltpu.make_async_copy(whole, whole, out_recv.at[chunk]).wait()
        others = state.at[chunk, pl.ds(0, boxes - 1)]
        pltpu.make_async_copy(others, others, out_send.at[chunk]).wait()


def local(n_bx, n_by, coeffs, interp, src_grid, tgt_grid):
    rows, width = coeffs.shape[1], coeffs.shape[-1]
    boxes = n_bx * n_by
    share = rows // boxes // CHUNKS
    anywhere = pl.BlockSpec(memory_space=pl.ANY)
    hbm = pl.BlockSpec(memory_space=pltpu.HBM)
    table = pltpu.VMEM((LEVELS, boxes, width), jnp.float32)
    dma = pltpu.SemaphoreType.DMA
    result = pl.pallas_call(
        functools.partial(kernel, n_bx, n_by),
        out_shape=jax.ShapeDtypeStruct((2, rows, width), coeffs.dtype),
        in_specs=[hbm] * 4,
        out_specs=anywhere,
        scratch_shapes=[
            pltpu.VMEM((CHUNKS, boxes, 2, share, width), coeffs.dtype),
            pltpu.VMEM((boxes, 2, share, width), coeffs.dtype),
            pltpu.VMEM(interp.shape, interp.dtype),
            pltpu.VMEM((LEVELS, n_by, n_bx), jnp.int32),
            pltpu.VMEM((1, width), jnp.int32),
            table,
            table,
            dma((CHUNKS, BATCHES)),
            dma((CHUNKS,)),
            dma((CHUNKS,)),
            dma((CHUNKS,)),
            dma((3,)),
        ],
        compiler_params=pltpu.CompilerParams(
            collective_id=0, has_side_effects=True, vmem_limit_bytes=48 * 1024 * 1024
        ),
        cost_estimate=pl.CostEstimate(
            flops=4 * LEVELS * coeffs.size * width, bytes_accessed=16 * 2**20, transcendentals=0
        ),
        name="butterfly",
    )(
        coeffs.reshape(2, rows, width),
        interp,
        pltpu.with_memory_space_constraint(tgt_grid.transpose(0, 2, 1), pltpu.HBM),
        pltpu.with_memory_space_constraint(src_grid.reshape(1, width), pltpu.HBM),
    )
    return result.reshape(2, rows, 1, 1, width)


def solution(mesh):
    placed = (P(None, None, "bx", "by", None), P(), P(), P())
    return jax.shard_map(
        functools.partial(local, mesh.shape["bx"], mesh.shape["by"]),
        mesh=mesh,
        in_specs=placed,
        out_specs=P(None, None, "bx", "by", None),
        check_vma=False,
    )
```

```python
import functools
import math

import jax
import jax.numpy as jnp
from jax import lax
from jax.experimental import pallas as pl
from jax.experimental.pallas import tpu as pltpu
from jax.sharding import PartitionSpec as P

GRID = 4096
LEVELS = 8
CHUNKS = 2
GROUP = 32
PAIRS = 16
SIDE = 4
BATCH = SIDE * SIDE
BATCHES = 2 * SIDE
EARLY = 6
MESH = pl.DeviceIdType.MESH


def level_bits(n_bx, n_by):
    bits_x = n_bx.bit_length() - 1
    bits_y = n_by.bit_length() - 1
    bits = []
    for level in range(LEVELS):
        if level % 2 == 0:
            bits.append(bits_y + level // 2 % bits_x)
        else:
            bits.append(level // 2 % bits_y)
    return bits


def phases(prod):
    quadrant = (prod + GRID // 8) >> 10
    angle = (prod - (quadrant << 10)).astype(jnp.float32) * (2.0 * math.pi / GRID)
    sq = angle * angle
    cosine = 1.0 + sq * (-1 / 2 + sq * (1 / 24 + sq * (-1 / 720 + sq * (1 / 40320))))
    sine = angle * (1.0 + sq * (-1 / 6 + sq * (1 / 120 + sq * (-1 / 5040 + sq * (1 / 362880)))))
    odd = (quadrant & 1) == 1
    first = jnp.where(odd, sine, cosine)
    second = jnp.where(odd, cosine, sine)
    cos_sign = jnp.where((quadrant == 1) | (quadrant == 2), -1.0, 1.0)
    sin_sign = jnp.where((quadrant == 2) | (quadrant == 3), -1.0, 1.0)
    return first * cos_sign, second * sin_sign


def apply_level(level, bit, source, target, interp, cosine, sine):
    boxes, _, rows, width = source.shape
    stride = 1 << bit
    weights = [interp[level, child].reshape(2 * width, width) for child in range(2)]
    weights = jnp.concatenate(weights, axis=1)

    def body(group, carry):
        if stride <= GROUP:
            low = [group * (2 * GROUP) + (i // stride * 2 * stride + i % stride) for i in range(GROUP)]
        else:
            runs = stride // GROUP
            base = group // runs * (2 * stride) + group % runs * GROUP
            low = [base + i for i in range(GROUP)]
        for begin in range(0, GROUP, PAIRS):
            some = low[begin:begin + PAIRS]
            halves = []
            for child in range(2):
                parts = [source[box + child * stride].reshape(2 * rows, width) for box in some]
                halves.append(jnp.concatenate(parts, axis=0))
            operand = jnp.concatenate(halves, axis=1)
            total = jnp.dot(operand, weights, preferred_element_type=jnp.float32)
            for i, box in enumerate(some):
                for child in range(2):
                    here = box + child * stride
                    re = total[2 * i * rows:(2 * i + 1) * rows, child * width:(child + 1) * width]
                    im = total[(2 * i + 1) * rows:(2 * i + 2) * rows, child * width:(child + 1) * width]
                    c = cosine[level, pl.ds(here, 1), :]
                    s = sine[level, pl.ds(here, 1), :]
                    target[here, 0] = (re * c - im * s).astype(jnp.bfloat16)
                    target[here, 1] = (re * s + im * c).astype(jnp.bfloat16)
        return carry

    lax.fori_loop(0, boxes // 2 // GROUP, body, 0)


def kernel(
    n_bx, n_by, coeffs, interp_hbm, tgt_hbm, src_hbm, out,
    state, spare, interp, tgt, src, cosine, sine, in_send, in_recv, out_send, out_recv, load_sem, heard,
):
    boxes = n_bx * n_by
    share = state.shape[3]
    bits = level_bits(n_bx, n_by)
    my_bx, my_by = lax.axis_index("bx"), lax.axis_index("by")
    me = my_bx * n_by + my_by
    my_x = my_bx // 4
    my_y = my_by // 4 * 2 + my_bx // 2 % 2
    my_z = my_by % 4
    my_core = my_bx % 2

    loads = [
        pltpu.make_async_copy(src_hbm, src, load_sem.at[0]),
        pltpu.make_async_copy(tgt_hbm, tgt, load_sem.at[1]),
        pltpu.make_async_copy(interp_hbm, interp, load_sem.at[2]),
    ]
    barrier = pltpu.get_barrier_semaphore()
    across = [((my_bx + i) % n_bx, my_by) for i in range(1, n_bx)]
    along = [(my_bx, (my_by + i) % n_by) for i in range(1, n_by)]
    for device in along + across:
        pl.semaphore_signal(barrier, inc=1, device_id=device, device_id_type=MESH)
    for load in loads:
        load.start()
    pl.semaphore_wait(barrier, len(along) + len(across))
    for device in across:
        pl.semaphore_signal(heard, inc=1, device_id=device, device_id_type=MESH)

    sign = 1 + (SIDE - 2) * my_core
    xs = [(my_x + sign * i) % SIDE * 4 for i in range(SIDE)]
    ys = [(my_y + sign * i) % SIDE for i in range(SIDE)]
    ys_bx = [y % 2 * 2 for y in ys]
    ys_by = [y // 2 * 4 for y in ys]

    def batch(number, visit):
        core = (my_core + number // SIDE) % 2
        bys = [ys_by[i] + (my_z + sign * (number + i)) % SIDE for i in range(SIDE)]
        for second in range(SIDE):
            for first in range(SIDE):
                if isinstance(number, int) and number == first == second == 0:
                    continue
                i = (first + second) % SIDE
                visit(xs[first] + ys_bx[i] + core, bys[i])

    def batches(start, stop, visit):
        if start == 0:
            batch(0, functools.partial(visit, 0))
            start = 1

        def body(number, carry):
            batch(number, functools.partial(visit, number))
            return carry

        lax.fori_loop(start, stop, body, 0)

    def rows_of(chunk, box):
        return pl.ds(pl.multiple_of((chunk * boxes + box) * share, share), share)

    def scatter(chunk, number, bx, by):
        pltpu.make_async_remote_copy(
            src_ref=coeffs.at[:, rows_of(chunk, bx * n_by + by)],
            dst_ref=state.at[chunk, me],
            send_sem=in_send.at[chunk, number],
            recv_sem=in_recv.at[chunk],
            device_id=(bx, by),
            device_id_type=MESH,
        ).start()

    def give_back(chunk, number, bx, by):
        pltpu.make_async_remote_copy(
            src_ref=state.at[chunk, bx * n_by + by],
            dst_ref=out.at[:, rows_of(chunk, me)],
            send_sem=out_send.at[chunk],
            recv_sem=out_recv.at[chunk],
            device_id=(bx, by),
            device_id_type=MESH,
        ).start()

    def wait_sent(chunk, number, count):
        sent = state.at[chunk, pl.ds(0, count)]
        pltpu.make_async_copy(sent, sent, in_send.at[chunk, number]).wait()

    pl.semaphore_wait(heard, len(across))
    batches(0, BATCHES, functools.partial(scatter, 0))
    for chunk in range(CHUNKS):
        pltpu.make_async_copy(coeffs.at[:, rows_of(chunk, me)], state.at[chunk, me], in_recv.at[chunk]).start()

    for load in loads:
        load.wait()

    def tables(level, carry):
        columns = tgt[level]
        for bx in range(n_bx):
            prod = (columns[:, bx:bx + 1] * src[...]) & (GRID - 1)
            here = pl.ds(bx * n_by, n_by)
            cosine[level, here, :], sine[level, here, :] = phases(prod)
        return carry

    lax.fori_loop(0, LEVELS, tables, 0)

    for number in range(EARLY):
        wait_sent(0, number, BATCH - (number == 0))
    batches(0, BATCHES // 2, functools.partial(scatter, 1))
    for number in range(EARLY, BATCHES):
        wait_sent(0, number, BATCH)
    batches(BATCHES // 2, BATCHES, functools.partial(scatter, 1))

    def work(chunk, carry):
        pltpu.make_async_copy(state.at[chunk], state.at[chunk], in_recv.at[chunk]).wait()

        for level in range(LEVELS):
            buffers = (state.at[chunk], spare)
            apply_level(level, bits[level], buffers[level % 2], buffers[1 - level % 2], interp, cosine, sine)
        pltpu.make_async_copy(state.at[chunk, me], out.at[:, rows_of(chunk, me)], out_recv.at[chunk]).start()
        batches(0, BATCHES, functools.partial(give_back, chunk))
        return carry

    lax.fori_loop(0, CHUNKS, work, 0)

    for number in range(BATCHES):
        wait_sent(1, number, BATCH - (number == 0))
    for chunk in range(CHUNKS):
        whole = out.at[:, pl.ds(chunk * boxes * share, boxes * share)]
        pltpu.make_async_copy(whole, whole, out_recv.at[chunk]).wait()
        others = state.at[chunk, pl.ds(0, boxes - 1)]
        pltpu.make_async_copy(others, others, out_send.at[chunk]).wait()


def local(n_bx, n_by, coeffs, interp, src_grid, tgt_grid):
    rows, width = coeffs.shape[1], coeffs.shape[-1]
    boxes = n_bx * n_by
    share = rows // boxes // CHUNKS
    anywhere = pl.BlockSpec(memory_space=pl.ANY)
    hbm = pl.BlockSpec(memory_space=pltpu.HBM)
    table = pltpu.VMEM((LEVELS, boxes, width), jnp.float32)
    dma = pltpu.SemaphoreType.DMA
    result = pl.pallas_call(
        functools.partial(kernel, n_bx, n_by),
        out_shape=jax.ShapeDtypeStruct((2, rows, width), coeffs.dtype),
        in_specs=[hbm] * 4,
        out_specs=anywhere,
        scratch_shapes=[
            pltpu.VMEM((CHUNKS, boxes, 2, share, width), coeffs.dtype),
            pltpu.VMEM((boxes, 2, share, width), coeffs.dtype),
            pltpu.VMEM(interp.shape, interp.dtype),
            pltpu.VMEM((LEVELS, n_by, n_bx), jnp.int32),
            pltpu.VMEM((1, width), jnp.int32),
            table,
            table,
            dma((CHUNKS, BATCHES)),
            dma((CHUNKS,)),
            dma((CHUNKS,)),
            dma((CHUNKS,)),
            dma((3,)),
            pltpu.SemaphoreType.REGULAR,
        ],
        compiler_params=pltpu.CompilerParams(
            collective_id=0, has_side_effects=True, vmem_limit_bytes=48 * 1024 * 1024
        ),
        cost_estimate=pl.CostEstimate(
            flops=4 * LEVELS * coeffs.size * width, bytes_accessed=16 * 2**20, transcendentals=0
        ),
        name="butterfly",
    )(
        coeffs.reshape(2, rows, width),
        interp,
        pltpu.with_memory_space_constraint(tgt_grid.transpose(0, 2, 1), pltpu.HBM),
        pltpu.with_memory_space_constraint(src_grid.reshape(1, width), pltpu.HBM),
    )
    return result.reshape(2, rows, 1, 1, width)


def solution(mesh):
    placed = (P(None, None, "bx", "by", None), P(), P(), P())
    return jax.shard_map(
        functools.partial(local, mesh.shape["bx"], mesh.shape["by"]),
        mesh=mesh,
        in_specs=placed,
        out_specs=P(None, None, "bx", "by", None),
        check_vma=False,
    )
```

```python
import functools
import math

import jax
import jax.numpy as jnp
from jax import lax
from jax.experimental import pallas as pl
from jax.experimental.pallas import tpu as pltpu
from jax.sharding import PartitionSpec as P

GRID = 4096
LEVELS = 8
CHUNKS = 2
GROUP = 32
PAIRS = 16
SIDE = 4
BATCH = SIDE * SIDE
BATCHES = 2 * SIDE
EARLY = 6
MESH = pl.DeviceIdType.MESH


def level_bits(n_bx, n_by):
    bits_x = n_bx.bit_length() - 1
    bits_y = n_by.bit_length() - 1
    bits = []
    for level in range(LEVELS):
        if level % 2 == 0:
            bits.append(bits_y + level // 2 % bits_x)
        else:
            bits.append(level // 2 % bits_y)
    return bits


def phases(prod):
    quadrant = (prod + GRID // 8) >> 10
    angle = (prod - (quadrant << 10)).astype(jnp.float32) * (2.0 * math.pi / GRID)
    sq = angle * angle
    cosine = 1.0 + sq * (-1 / 2 + sq * (1 / 24 + sq * (-1 / 720 + sq * (1 / 40320))))
    sine = angle * (1.0 + sq * (-1 / 6 + sq * (1 / 120 + sq * (-1 / 5040 + sq * (1 / 362880)))))
    odd = (quadrant & 1) == 1
    first = jnp.where(odd, sine, cosine)
    second = jnp.where(odd, cosine, sine)
    cos_sign = jnp.where((quadrant == 1) | (quadrant == 2), -1.0, 1.0)
    sin_sign = jnp.where((quadrant == 2) | (quadrant == 3), -1.0, 1.0)
    return first * cos_sign, second * sin_sign


def apply_level(level, bit, source, target, interp, cosine, sine):
    boxes, _, rows, width = source.shape
    stride = 1 << bit
    weights = [interp[level, child].reshape(2 * width, width) for child in range(2)]
    weights = jnp.concatenate(weights, axis=1)

    def body(group, carry):
        if stride <= GROUP:
            low = [group * (2 * GROUP) + (i // stride * 2 * stride + i % stride) for i in range(GROUP)]
        else:
            runs = stride // GROUP
            base = group // runs * (2 * stride) + group % runs * GROUP
            low = [base + i for i in range(GROUP)]
        for begin in range(0, GROUP, PAIRS):
            some = low[begin:begin + PAIRS]
            halves = []
            for child in range(2):
                parts = [source[box + child * stride].reshape(2 * rows, width) for box in some]
                halves.append(jnp.concatenate(parts, axis=0))
            operand = jnp.concatenate(halves, axis=1)
            total = jnp.dot(operand, weights, preferred_element_type=jnp.float32)
            for i, box in enumerate(some):
                for child in range(2):
                    here = box + child * stride
                    re = total[2 * i * rows:(2 * i + 1) * rows, child * width:(child + 1) * width]
                    im = total[(2 * i + 1) * rows:(2 * i + 2) * rows, child * width:(child + 1) * width]
                    c = cosine[level, pl.ds(here, 1), :]
                    s = sine[level, pl.ds(here, 1), :]
                    target[here, 0] = (re * c - im * s).astype(jnp.bfloat16)
                    target[here, 1] = (re * s + im * c).astype(jnp.bfloat16)
        return carry

    lax.fori_loop(0, boxes // 2 // GROUP, body, 0)


def kernel(
    n_bx, n_by, coeffs, interp_hbm, tgt_hbm, src_hbm, out,
    staged, state, spare, interp, tgt, src, cosine, sine, in_send, in_recv, out_send, out_recv, load_sem, stage_sem, heard,
):
    boxes = n_bx * n_by
    share = state.shape[3]
    bits = level_bits(n_bx, n_by)
    my_bx, my_by = lax.axis_index("bx"), lax.axis_index("by")
    me = my_bx * n_by + my_by
    my_x = my_bx // 4
    my_y = my_by // 4 * 2 + my_bx // 2 % 2
    my_z = my_by % 4
    my_core = my_bx % 2

    loads = [
        pltpu.make_async_copy(src_hbm, src, load_sem.at[0]),
        pltpu.make_async_copy(tgt_hbm, tgt, load_sem.at[1]),
        pltpu.make_async_copy(interp_hbm, interp, load_sem.at[2]),
    ]
    halves = [
        pltpu.make_async_copy(
            coeffs.at[:, pl.ds(chunk * boxes * share, boxes * share)],
            staged.at[:, pl.ds(chunk * boxes * share, boxes * share)],
            stage_sem.at[chunk],
        )
        for chunk in range(CHUNKS)
    ]

    barrier = pltpu.get_barrier_semaphore()
    across = [((my_bx + i) % n_bx, my_by) for i in range(1, n_bx)]
    along = [(my_bx, (my_by + i) % n_by) for i in range(1, n_by)]
    for device in along + across:
        pl.semaphore_signal(barrier, inc=1, device_id=device, device_id_type=MESH)
    for load in halves + loads:
        load.start()
    pl.semaphore_wait(barrier, len(along) + len(across))
    for device in across:
        pl.semaphore_signal(heard, inc=1, device_id=device, device_id_type=MESH)

    sign = 1 + (SIDE - 2) * my_core
    xs = [(my_x + sign * i) % SIDE * 4 for i in range(SIDE)]
    ys = [(my_y + sign * i) % SIDE for i in range(SIDE)]
    ys_bx = [y % 2 * 2 for y in ys]
    ys_by = [y // 2 * 4 for y in ys]

    def batch(number, visit):
        core = (my_core + number // SIDE) % 2
        bys = [ys_by[i] + (my_z + sign * (number + i)) % SIDE for i in range(SIDE)]
        for second in range(SIDE):
            for first in range(SIDE):
                if isinstance(number, int) and number == first == second == 0:
                    continue
                i = (first + second) % SIDE
                visit(first % 2, xs[first] + ys_bx[i] + core, bys[i])

    def batches(start, stop, visit):
        if start == 0:
            batch(0, functools.partial(visit, 0))
            start = 1

        def body(number, carry):
            batch(number, functools.partial(visit, number))
            return carry

        lax.fori_loop(start, stop, body, 0)

    def rows_of(chunk, box):
        return pl.ds(pl.multiple_of((chunk * boxes + box) * share, share), share)

    def scatter(chunk, number, odd, bx, by):
        pltpu.make_async_remote_copy(
            src_ref=(staged if odd else coeffs).at[:, rows_of(chunk, bx * n_by + by)],
            dst_ref=state.at[chunk, me],
            send_sem=in_send.at[chunk, number],
            recv_sem=in_recv.at[chunk],
            device_id=(bx, by),
            device_id_type=MESH,
        ).start()

    def give_back(chunk, number, odd, bx, by):
        pltpu.make_async_remote_copy(
            src_ref=state.at[chunk, bx * n_by + by],
            dst_ref=out.at[:, rows_of(chunk, me)],
            send_sem=out_send.at[chunk],
            recv_sem=out_recv.at[chunk],
            device_id=(bx, by),
            device_id_type=MESH,
        ).start()

    def wait_sent(chunk, number, count):
        sent = state.at[chunk, pl.ds(0, count)]
        pltpu.make_async_copy(sent, sent, in_send.at[chunk, number]).wait()

    pl.semaphore_wait(heard, len(across))
    halves[0].wait()
    batches(0, BATCHES, functools.partial(scatter, 0))
    halves[1].wait()
    for chunk in range(CHUNKS):
        pltpu.make_async_copy(coeffs.at[:, rows_of(chunk, me)], state.at[chunk, me], in_recv.at[chunk]).start()

    for load in loads:
        load.wait()

    def tables(level, carry):
        columns = tgt[level]
        for bx in range(n_bx):
            prod = (columns[:, bx:bx + 1] * src[...]) & (GRID - 1)
            here = pl.ds(bx * n_by, n_by)
            cosine[level, here, :], sine[level, here, :] = phases(prod)
        return carry

    lax.fori_loop(0, LEVELS, tables, 0)

    for number in range(EARLY):
        wait_sent(0, number, BATCH - (number == 0))
    batches(0, BATCHES // 2, functools.partial(scatter, 1))
    for number in range(EARLY, BATCHES):
        wait_sent(0, number, BATCH)
    batches(BATCHES // 2, BATCHES, functools.partial(scatter, 1))

    def work(chunk, carry):
        pltpu.make_async_copy(state.at[chunk], state.at[chunk], in_recv.at[chunk]).wait()

        for level in range(LEVELS):
            buffers = (state.at[chunk], spare)
            apply_level(level, bits[level], buffers[level % 2], buffers[1 - level % 2], interp, cosine, sine)
        pltpu.make_async_copy(state.at[chunk, me], out.at[:, rows_of(chunk, me)], out_recv.at[chunk]).start()
        batches(0, BATCHES, functools.partial(give_back, chunk))
        return carry

    lax.fori_loop(0, CHUNKS, work, 0)

    for number in range(BATCHES):
        wait_sent(1, number, BATCH - (number == 0))
    for chunk in range(CHUNKS):
        whole = out.at[:, pl.ds(chunk * boxes * share, boxes * share)]
        pltpu.make_async_copy(whole, whole, out_recv.at[chunk]).wait()
        others = state.at[chunk, pl.ds(0, boxes - 1)]
        pltpu.make_async_copy(others, others, out_send.at[chunk]).wait()


def local(n_bx, n_by, coeffs, interp, src_grid, tgt_grid):
    rows, width = coeffs.shape[1], coeffs.shape[-1]
    boxes = n_bx * n_by
    share = rows // boxes // CHUNKS
    anywhere = pl.BlockSpec(memory_space=pl.ANY)
    hbm = pl.BlockSpec(memory_space=pltpu.HBM)
    table = pltpu.VMEM((LEVELS, boxes, width), jnp.float32)
    dma = pltpu.SemaphoreType.DMA
    result = pl.pallas_call(
        functools.partial(kernel, n_bx, n_by),
        out_shape=jax.ShapeDtypeStruct((2, rows, width), coeffs.dtype),
        in_specs=[hbm] * 4,
        out_specs=anywhere,
        scratch_shapes=[
            pltpu.VMEM((2, rows, width), coeffs.dtype),
            pltpu.VMEM((CHUNKS, boxes, 2, share, width), coeffs.dtype),
            pltpu.VMEM((boxes, 2, share, width), coeffs.dtype),
            pltpu.VMEM(interp.shape, interp.dtype),
            pltpu.VMEM((LEVELS, n_by, n_bx), jnp.int32),
            pltpu.VMEM((1, width), jnp.int32),
            table,
            table,
            dma((CHUNKS, BATCHES)),
            dma((CHUNKS,)),
            dma((CHUNKS,)),
            dma((CHUNKS,)),
            dma((3,)),
            dma((CHUNKS,)),
            pltpu.SemaphoreType.REGULAR,
        ],
        compiler_params=pltpu.CompilerParams(
            collective_id=0, has_side_effects=True, vmem_limit_bytes=48 * 1024 * 1024
        ),
        cost_estimate=pl.CostEstimate(
            flops=4 * LEVELS * coeffs.size * width, bytes_accessed=16 * 2**20, transcendentals=0
        ),
        name="butterfly",
    )(
        coeffs.reshape(2, rows, width),
        interp,
        pltpu.with_memory_space_constraint(tgt_grid.transpose(0, 2, 1), pltpu.HBM),
        pltpu.with_memory_space_constraint(src_grid.reshape(1, width), pltpu.HBM),
    )
    return result.reshape(2, rows, 1, 1, width)


def solution(mesh):
    placed = (P(None, None, "bx", "by", None), P(), P(), P())
    return jax.shard_map(
        functools.partial(local, mesh.shape["bx"], mesh.shape["by"]),
        mesh=mesh,
        in_specs=placed,
        out_specs=P(None, None, "bx", "by", None),
        check_vma=False,
    )
```

```python
import functools
import math

import jax
import jax.numpy as jnp
from jax import lax
from jax.experimental import pallas as pl
from jax.experimental.pallas import tpu as pltpu
from jax.sharding import PartitionSpec as P

GRID = 4096
LEVELS = 8
CHUNKS = 2
GROUP = 32
PAIRS = 16
SIDE = 4
BATCH = SIDE * SIDE
BATCHES = 2 * SIDE
EARLY = 6
MESH = pl.DeviceIdType.MESH


def level_bits(n_bx, n_by):
    bits_x = n_bx.bit_length() - 1
    bits_y = n_by.bit_length() - 1
    bits = []
    for level in range(LEVELS):
        if level % 2 == 0:
            bits.append(bits_y + level // 2 % bits_x)
        else:
            bits.append(level // 2 % bits_y)
    return bits


def phases(prod):
    quadrant = (prod + GRID // 8) >> 10
    angle = (prod - (quadrant << 10)).astype(jnp.float32) * (2.0 * math.pi / GRID)
    sq = angle * angle
    cosine = 1.0 + sq * (-1 / 2 + sq * (1 / 24 + sq * (-1 / 720 + sq * (1 / 40320))))
    sine = angle * (1.0 + sq * (-1 / 6 + sq * (1 / 120 + sq * (-1 / 5040 + sq * (1 / 362880)))))
    odd = (quadrant & 1) == 1
    first = jnp.where(odd, sine, cosine)
    second = jnp.where(odd, cosine, sine)
    cos_sign = jnp.where((quadrant == 1) | (quadrant == 2), -1.0, 1.0)
    sin_sign = jnp.where((quadrant == 2) | (quadrant == 3), -1.0, 1.0)
    return first * cos_sign, second * sin_sign


def apply_level(level, bit, source, target, interp, cosine, sine):
    boxes, _, rows, width = source.shape
    stride = 1 << bit
    weights = [interp[level, child].reshape(2 * width, width) for child in range(2)]
    weights = jnp.concatenate(weights, axis=1)

    def body(group, carry):
        if stride <= GROUP:
            low = [group * (2 * GROUP) + (i // stride * 2 * stride + i % stride) for i in range(GROUP)]
        else:
            runs = stride // GROUP
            base = group // runs * (2 * stride) + group % runs * GROUP
            low = [base + i for i in range(GROUP)]
        for begin in range(0, GROUP, PAIRS):
            some = low[begin:begin + PAIRS]
            halves = []
            for child in range(2):
                parts = [source[box + child * stride].reshape(2 * rows, width) for box in some]
                halves.append(jnp.concatenate(parts, axis=0))
            operand = jnp.concatenate(halves, axis=1)
            total = jnp.dot(operand, weights, preferred_element_type=jnp.float32)
            for i, box in enumerate(some):
                for child in range(2):
                    here = box + child * stride
                    re = total[2 * i * rows:(2 * i + 1) * rows, child * width:(child + 1) * width]
                    im = total[(2 * i + 1) * rows:(2 * i + 2) * rows, child * width:(child + 1) * width]
                    c = cosine[level, pl.ds(here, 1), :]
                    s = sine[level, pl.ds(here, 1), :]
                    target[here, 0] = (re * c - im * s).astype(jnp.bfloat16)
                    target[here, 1] = (re * s + im * c).astype(jnp.bfloat16)
        return carry

    lax.fori_loop(0, boxes // 2 // GROUP, body, 0)


def kernel(
    n_bx, n_by, coeffs, interp_hbm, tgt_hbm, src_hbm, out,
    state, spare, interp, tgt, src, cosine, sine, in_send, in_recv, out_send, out_recv, load_sem, heard,
):
    boxes = n_bx * n_by
    share = state.shape[3]
    bits = level_bits(n_bx, n_by)
    my_bx, my_by = lax.axis_index("bx"), lax.axis_index("by")
    me = my_bx * n_by + my_by
    my_x = my_bx // 4
    my_y = my_by // 4 * 2 + my_bx // 2 % 2
    my_z = my_by % 4
    my_core = my_bx % 2

    loads = [
        pltpu.make_async_copy(src_hbm, src, load_sem.at[0]),
        pltpu.make_async_copy(tgt_hbm, tgt, load_sem.at[1]),
        pltpu.make_async_copy(interp_hbm, interp, load_sem.at[2]),
    ]
    sign = 1 + (SIDE - 2) * my_core
    xs = [(my_x + sign * i) % SIDE * 4 for i in range(SIDE)]
    ys = [(my_y + sign * i) % SIDE for i in range(SIDE)]
    ys_bx = [y % 2 * 2 for y in ys]
    ys_by = [y // 2 * 4 for y in ys]

    zs = [(my_z + sign * i) % SIDE for i in range(SIDE)]
    line = [(xs[i] + ys_bx[0] + (my_core + j) % 2, my_by) for j in range(2) for i in range(SIDE)][1:]
    plane = [
        (xs[0] + ys_bx[i] + my_core, ys_by[i] + zs[(i + j) % SIDE]) for j in range(SIDE) for i in range(SIDE)
    ][1:]
    barrier = pltpu.get_barrier_semaphore()
    for device in plane + line:
        pl.semaphore_signal(barrier, inc=1, device_id=device, device_id_type=MESH)
    for load in loads:
        load.start()
    pl.semaphore_wait(barrier, len(plane) + len(line))
    for device in line:
        pl.semaphore_signal(heard, inc=1, device_id=device, device_id_type=MESH)

    def on_line_or_plane(number, first, second):
        return (number < SIDE and first == 0) or (number % SIDE == 0 and (first + second) % SIDE == 0)

    def batch(number, visit, skip=None):
        core = (my_core + number // SIDE) % 2
        bys = [ys_by[i] + (my_z + sign * (number + i)) % SIDE for i in range(SIDE)]
        for second in range(SIDE):
            for first in range(SIDE):
                if isinstance(number, int) and number == first == second == 0:
                    continue
                if skip is not None and skip(number, first, second):
                    continue
                i = (first + second) % SIDE
                visit(xs[first] + ys_bx[i] + core, bys[i])

    def batches(start, stop, visit):
        if start == 0:
            batch(0, functools.partial(visit, 0))
            start = 1

        def body(number, carry):
            batch(number, functools.partial(visit, number))
            return carry

        lax.fori_loop(start, stop, body, 0)

    def rows_of(chunk, box):
        return pl.ds(pl.multiple_of((chunk * boxes + box) * share, share), share)

    def scatter(chunk, number, bx, by):
        pltpu.make_async_remote_copy(
            src_ref=coeffs.at[:, rows_of(chunk, bx * n_by + by)],
            dst_ref=state.at[chunk, me],
            send_sem=in_send.at[chunk, number],
            recv_sem=in_recv.at[chunk],
            device_id=(bx, by),
            device_id_type=MESH,
        ).start()

    def give_back(chunk, number, bx, by):
        pltpu.make_async_remote_copy(
            src_ref=state.at[chunk, bx * n_by + by],
            dst_ref=out.at[:, rows_of(chunk, me)],
            send_sem=out_send.at[chunk],
            recv_sem=out_recv.at[chunk],
            device_id=(bx, by),
            device_id_type=MESH,
        ).start()

    def wait_sent(chunk, number, count):
        sent = state.at[chunk, pl.ds(0, count)]
        pltpu.make_async_copy(sent, sent, in_send.at[chunk, number]).wait()

    for i in range(len(plane)):
        scatter(0, BATCHES, *plane[i])
        if i % 2 == 1:
            scatter(0, BATCHES, *line[i // 2])
    pl.semaphore_wait(heard, len(line))
    for number in range(BATCHES):
        batch(number, functools.partial(scatter, 0, number), on_line_or_plane)
    for chunk in range(CHUNKS):
        pltpu.make_async_copy(coeffs.at[:, rows_of(chunk, me)], state.at[chunk, me], in_recv.at[chunk]).start()

    for load in loads:
        load.wait()

    def tables(level, carry):
        columns = tgt[level]
        for bx in range(n_bx):
            prod = (columns[:, bx:bx + 1] * src[...]) & (GRID - 1)
            here = pl.ds(bx * n_by, n_by)
            cosine[level, here, :], sine[level, here, :] = phases(prod)
        return carry

    lax.fori_loop(0, LEVELS, tables, 0)

    counts = [
        sum(not on_line_or_plane(number, i, j) for i in range(SIDE) for j in range(SIDE)) for number in range(BATCHES)
    ]
    wait_sent(0, BATCHES, len(plane) + len(line))
    for number in range(EARLY):
        wait_sent(0, number, counts[number])
    batches(0, BATCHES // 2, functools.partial(scatter, 1))
    for number in range(EARLY, BATCHES):
        wait_sent(0, number, counts[number])
    batches(BATCHES // 2, BATCHES, functools.partial(scatter, 1))

    def work(chunk, carry):
        pltpu.make_async_copy(state.at[chunk], state.at[chunk], in_recv.at[chunk]).wait()

        for level in range(LEVELS):
            buffers = (state.at[chunk], spare)
            apply_level(level, bits[level], buffers[level % 2], buffers[1 - level % 2], interp, cosine, sine)
        pltpu.make_async_copy(state.at[chunk, me], out.at[:, rows_of(chunk, me)], out_recv.at[chunk]).start()
        batches(0, BATCHES, functools.partial(give_back, chunk))
        return carry

    lax.fori_loop(0, CHUNKS, work, 0)

    for number in range(BATCHES):
        wait_sent(1, number, BATCH - (number == 0))
    for chunk in range(CHUNKS):
        whole = out.at[:, pl.ds(chunk * boxes * share, boxes * share)]
        pltpu.make_async_copy(whole, whole, out_recv.at[chunk]).wait()
        others = state.at[chunk, pl.ds(0, boxes - 1)]
        pltpu.make_async_copy(others, others, out_send.at[chunk]).wait()


def local(n_bx, n_by, coeffs, interp, src_grid, tgt_grid):
    rows, width = coeffs.shape[1], coeffs.shape[-1]
    boxes = n_bx * n_by
    share = rows // boxes // CHUNKS
    anywhere = pl.BlockSpec(memory_space=pl.ANY)
    hbm = pl.BlockSpec(memory_space=pltpu.HBM)
    table = pltpu.VMEM((LEVELS, boxes, width), jnp.float32)
    dma = pltpu.SemaphoreType.DMA
    result = pl.pallas_call(
        functools.partial(kernel, n_bx, n_by),
        out_shape=jax.ShapeDtypeStruct((2, rows, width), coeffs.dtype),
        in_specs=[hbm] * 4,
        out_specs=anywhere,
        scratch_shapes=[
            pltpu.VMEM((CHUNKS, boxes, 2, share, width), coeffs.dtype),
            pltpu.VMEM((boxes, 2, share, width), coeffs.dtype),
            pltpu.VMEM(interp.shape, interp.dtype),
            pltpu.VMEM((LEVELS, n_by, n_bx), jnp.int32),
            pltpu.VMEM((1, width), jnp.int32),
            table,
            table,
            dma((CHUNKS, BATCHES + 1)),
            dma((CHUNKS,)),
            dma((CHUNKS,)),
            dma((CHUNKS,)),
            dma((3,)),
            pltpu.SemaphoreType.REGULAR,
        ],
        compiler_params=pltpu.CompilerParams(
            collective_id=0, has_side_effects=True, vmem_limit_bytes=48 * 1024 * 1024
        ),
        cost_estimate=pl.CostEstimate(
            flops=4 * LEVELS * coeffs.size * width, bytes_accessed=16 * 2**20, transcendentals=0
        ),
        name="butterfly",
    )(
        coeffs.reshape(2, rows, width),
        interp,
        pltpu.with_memory_space_constraint(tgt_grid.transpose(0, 2, 1), pltpu.HBM),
        pltpu.with_memory_space_constraint(src_grid.reshape(1, width), pltpu.HBM),
    )
    return result.reshape(2, rows, 1, 1, width)


def solution(mesh):
    placed = (P(None, None, "bx", "by", None), P(), P(), P())
    return jax.shard_map(
        functools.partial(local, mesh.shape["bx"], mesh.shape["by"]),
        mesh=mesh,
        in_specs=placed,
        out_specs=P(None, None, "bx", "by", None),
        check_vma=False,
    )
```

```python
import functools
import math

import jax
import jax.numpy as jnp
from jax import lax
from jax.experimental import pallas as pl
from jax.experimental.pallas import tpu as pltpu
from jax.sharding import PartitionSpec as P

GRID = 4096
LEVELS = 8
CHUNKS = 2
GROUP = 32
PAIRS = 16
SIDE = 4
BATCH = SIDE * SIDE
BATCHES = 2 * SIDE
EARLY = 4
MESH = pl.DeviceIdType.MESH


def level_bits(n_bx, n_by):
    bits_x = n_bx.bit_length() - 1
    bits_y = n_by.bit_length() - 1
    bits = []
    for level in range(LEVELS):
        if level % 2 == 0:
            bits.append(bits_y + level // 2 % bits_x)
        else:
            bits.append(level // 2 % bits_y)
    return bits


def phases(prod):
    quadrant = (prod + GRID // 8) >> 10
    angle = (prod - (quadrant << 10)).astype(jnp.float32) * (2.0 * math.pi / GRID)
    sq = angle * angle
    cosine = 1.0 + sq * (-1 / 2 + sq * (1 / 24 + sq * (-1 / 720 + sq * (1 / 40320))))
    sine = angle * (1.0 + sq * (-1 / 6 + sq * (1 / 120 + sq * (-1 / 5040 + sq * (1 / 362880)))))
    odd = (quadrant & 1) == 1
    first = jnp.where(odd, sine, cosine)
    second = jnp.where(odd, cosine, sine)
    cos_sign = jnp.where((quadrant == 1) | (quadrant == 2), -1.0, 1.0)
    sin_sign = jnp.where((quadrant == 2) | (quadrant == 3), -1.0, 1.0)
    return first * cos_sign, second * sin_sign


def apply_level(level, bit, source, target, interp, cosine, sine):
    boxes, _, rows, width = source.shape
    stride = 1 << bit
    weights = [interp[level, child].reshape(2 * width, width) for child in range(2)]
    weights = jnp.concatenate(weights, axis=1)

    def body(group, carry):
        if stride <= GROUP:
            low = [group * (2 * GROUP) + (i // stride * 2 * stride + i % stride) for i in range(GROUP)]
        else:
            runs = stride // GROUP
            base = group // runs * (2 * stride) + group % runs * GROUP
            low = [base + i for i in range(GROUP)]
        for begin in range(0, GROUP, PAIRS):
            some = low[begin:begin + PAIRS]
            halves = []
            for child in range(2):
                parts = [source[box + child * stride].reshape(2 * rows, width) for box in some]
                halves.append(jnp.concatenate(parts, axis=0))
            operand = jnp.concatenate(halves, axis=1)
            total = jnp.dot(operand, weights, preferred_element_type=jnp.float32)
            for i, box in enumerate(some):
                for child in range(2):
                    here = box + child * stride
                    re = total[2 * i * rows:(2 * i + 1) * rows, child * width:(child + 1) * width]
                    im = total[(2 * i + 1) * rows:(2 * i + 2) * rows, child * width:(child + 1) * width]
                    c = cosine[level, pl.ds(here, 1), :]
                    s = sine[level, pl.ds(here, 1), :]
                    target[here, 0] = (re * c - im * s).astype(jnp.bfloat16)
                    target[here, 1] = (re * s + im * c).astype(jnp.bfloat16)
        return carry

    lax.fori_loop(0, boxes // 2 // GROUP, body, 0)


def offsets_by_distance():
    hops = (0, 1, 2, 1)
    rings = [[] for _ in range(7)]
    load = [0] * 6
    steps = range(SIDE)
    everyone = [(dx, dy, dz, core) for core in range(2) for dz in steps for dy in steps for dx in steps]

    def added(offset):
        total = list(load)
        for axis in range(3):
            total[2 * axis] += offset[axis] in (1, 2)
            total[2 * axis + 1] += offset[axis] in (2, 3)
        return total

    for ring in range(7):
        left = [o for o in everyone if hops[o[0]] + hops[o[1]] + hops[o[2]] + o[3] == ring + 1]
        while left:
            best = min(left, key=lambda o: sum(t * t for t in added(o)) - 2 * sum(load) * sum(added(o)) / 6)
            left.remove(best)
            load = added(best)
            rings[ring].append(best)
    return rings


def kernel(
    n_bx, n_by, coeffs, interp_hbm, tgt_hbm, src_hbm, out,
    state, spare, interp, tgt, src, cosine, sine, in_send, in_recv, out_send, out_recv, load_sem, heard,
):
    boxes = n_bx * n_by
    share = state.shape[3]
    bits = level_bits(n_bx, n_by)
    my_bx, my_by = lax.axis_index("bx"), lax.axis_index("by")
    me = my_bx * n_by + my_by
    my_x = my_bx // 4
    my_y = my_by // 4 * 2 + my_bx // 2 % 2
    my_z = my_by % 4
    my_core = my_bx % 2

    loads = [
        pltpu.make_async_copy(src_hbm, src, load_sem.at[0]),
        pltpu.make_async_copy(tgt_hbm, tgt, load_sem.at[1]),
        pltpu.make_async_copy(interp_hbm, interp, load_sem.at[2]),
    ]
    sign = 1 + (SIDE - 2) * my_core
    xs = [(my_x + sign * i) % SIDE * 4 for i in range(SIDE)]
    ys = [(my_y + sign * i) % SIDE for i in range(SIDE)]
    ys_bx = [y % 2 * 2 for y in ys]
    ys_by = [y // 2 * 4 for y in ys]

    zs = [(my_z + sign * i) % SIDE for i in range(SIDE)]
    def peer(offset):
        dx, dy, dz, core = offset
        return xs[dx] + ys_bx[dy] + (my_core + core) % 2, ys_by[dy] + zs[dz]

    def batch(number, visit):
        core = (my_core + number // SIDE) % 2
        bys = [ys_by[i] + (my_z + sign * (number + i)) % SIDE for i in range(SIDE)]
        for second in range(SIDE):
            for first in range(SIDE):
                if isinstance(number, int) and number == first == second == 0:
                    continue
                i = (first + second) % SIDE
                visit(xs[first] + ys_bx[i] + core, bys[i])

    def batches(start, stop, visit):
        if start == 0:
            batch(0, functools.partial(visit, 0))
            start = 1

        def body(number, carry):
            batch(number, functools.partial(visit, number))
            return carry

        lax.fori_loop(start, stop, body, 0)

    def rows_of(chunk, box):
        return pl.ds(pl.multiple_of((chunk * boxes + box) * share, share), share)

    def scatter(chunk, number, bx, by):
        pltpu.make_async_remote_copy(
            src_ref=coeffs.at[:, rows_of(chunk, bx * n_by + by)],
            dst_ref=state.at[chunk, me],
            send_sem=in_send.at[chunk, number],
            recv_sem=in_recv.at[chunk],
            device_id=(bx, by),
            device_id_type=MESH,
        ).start()

    def give_back(chunk, number, bx, by):
        pltpu.make_async_remote_copy(
            src_ref=state.at[chunk, bx * n_by + by],
            dst_ref=out.at[:, rows_of(chunk, me)],
            send_sem=out_send.at[chunk],
            recv_sem=out_recv.at[chunk],
            device_id=(bx, by),
            device_id_type=MESH,
        ).start()

    def wait_sent(chunk, number, count):
        sent = state.at[chunk, pl.ds(0, count)]
        pltpu.make_async_copy(sent, sent, in_send.at[chunk, number]).wait()

    rings = offsets_by_distance()
    near = [peer(offset) for offset in rings[0]]
    barrier = pltpu.get_barrier_semaphore()
    for device in near:
        pl.semaphore_signal(barrier, inc=1, device_id=device, device_id_type=MESH)
    for load in loads:
        load.start()
    for ring, offsets in enumerate(rings):
        pl.semaphore_wait(barrier if ring == 0 else heard.at[ring], len(near))
        if ring < len(rings) - 1:
            for device in near:
                pl.semaphore_signal(heard.at[ring + 1], inc=1, device_id=device, device_id_type=MESH)
        for offset in offsets:
            scatter(0, ring, *peer(offset))
    for chunk in range(CHUNKS):
        pltpu.make_async_copy(coeffs.at[:, rows_of(chunk, me)], state.at[chunk, me], in_recv.at[chunk]).start()

    for load in loads:
        load.wait()

    def tables(level, carry):
        columns = tgt[level]
        for bx in range(n_bx):
            prod = (columns[:, bx:bx + 1] * src[...]) & (GRID - 1)
            here = pl.ds(bx * n_by, n_by)
            cosine[level, here, :], sine[level, here, :] = phases(prod)
        return carry

    lax.fori_loop(0, LEVELS, tables, 0)

    for ring in range(EARLY):
        wait_sent(0, ring, len(rings[ring]))
    batches(0, BATCHES // 2, functools.partial(scatter, 1))
    for ring in range(EARLY, len(rings)):
        wait_sent(0, ring, len(rings[ring]))
    batches(BATCHES // 2, BATCHES, functools.partial(scatter, 1))

    def work(chunk, carry):
        pltpu.make_async_copy(state.at[chunk], state.at[chunk], in_recv.at[chunk]).wait()

        for level in range(LEVELS):
            buffers = (state.at[chunk], spare)
            apply_level(level, bits[level], buffers[level % 2], buffers[1 - level % 2], interp, cosine, sine)
        pltpu.make_async_copy(state.at[chunk, me], out.at[:, rows_of(chunk, me)], out_recv.at[chunk]).start()
        batches(0, BATCHES, functools.partial(give_back, chunk))
        return carry

    lax.fori_loop(0, CHUNKS, work, 0)

    for number in range(BATCHES):
        wait_sent(1, number, BATCH - (number == 0))
    for chunk in range(CHUNKS):
        whole = out.at[:, pl.ds(chunk * boxes * share, boxes * share)]
        pltpu.make_async_copy(whole, whole, out_recv.at[chunk]).wait()
        others = state.at[chunk, pl.ds(0, boxes - 1)]
        pltpu.make_async_copy(others, others, out_send.at[chunk]).wait()


def local(n_bx, n_by, coeffs, interp, src_grid, tgt_grid):
    rows, width = coeffs.shape[1], coeffs.shape[-1]
    boxes = n_bx * n_by
    share = rows // boxes // CHUNKS
    anywhere = pl.BlockSpec(memory_space=pl.ANY)
    hbm = pl.BlockSpec(memory_space=pltpu.HBM)
    table = pltpu.VMEM((LEVELS, boxes, width), jnp.float32)
    dma = pltpu.SemaphoreType.DMA
    result = pl.pallas_call(
        functools.partial(kernel, n_bx, n_by),
        out_shape=jax.ShapeDtypeStruct((2, rows, width), coeffs.dtype),
        in_specs=[hbm] * 4,
        out_specs=anywhere,
        scratch_shapes=[
            pltpu.VMEM((CHUNKS, boxes, 2, share, width), coeffs.dtype),
            pltpu.VMEM((boxes, 2, share, width), coeffs.dtype),
            pltpu.VMEM(interp.shape, interp.dtype),
            pltpu.VMEM((LEVELS, n_by, n_bx), jnp.int32),
            pltpu.VMEM((1, width), jnp.int32),
            table,
            table,
            dma((CHUNKS, BATCHES)),
            dma((CHUNKS,)),
            dma((CHUNKS,)),
            dma((CHUNKS,)),
            dma((3,)),
            pltpu.SemaphoreType.REGULAR((7,)),
        ],
        compiler_params=pltpu.CompilerParams(
            collective_id=0, has_side_effects=True, vmem_limit_bytes=48 * 1024 * 1024
        ),
        cost_estimate=pl.CostEstimate(
            flops=4 * LEVELS * coeffs.size * width, bytes_accessed=16 * 2**20, transcendentals=0
        ),
        name="butterfly",
    )(
        coeffs.reshape(2, rows, width),
        interp,
        pltpu.with_memory_space_constraint(tgt_grid.transpose(0, 2, 1), pltpu.HBM),
        pltpu.with_memory_space_constraint(src_grid.reshape(1, width), pltpu.HBM),
    )
    return result.reshape(2, rows, 1, 1, width)


def solution(mesh):
    placed = (P(None, None, "bx", "by", None), P(), P(), P())
    return jax.shard_map(
        functools.partial(local, mesh.shape["bx"], mesh.shape["by"]),
        mesh=mesh,
        in_specs=placed,
        out_specs=P(None, None, "bx", "by", None),
        check_vma=False,
    )
```
